32 devices in a mesh: groups: 2 (over x), seq: 16 (over z, y, core).
Axes of the slice: x: 2, y: 2, z: 4, core: 2. Of those that a mesh axis runs over, the one named last changes fastest.
Arguments:
- queries: bfloat16 [8, 4096, 3072], P('groups', 'seq'), parts along dimension 0, may hold values from -28 to 28
- keys: bfloat16 [8, 4096, 3072], P('groups', 'seq'), parts along dimension 0, may hold values from -28 to 28
- values: bfloat16 [8, 4096, 3072], P('groups', 'seq'), parts along dimension 0, may hold values from -6 to 6
- tile_list: int32 [24, 16, 16], P(None, 'seq'), may hold values from 0 to 15, as said below
- head_counts: int32 [24], replicated, may hold values from 4 to 16
Outputs:
- attended: bfloat16 [8, 4096, 3072], P('groups', 'seq'), parts along dimension 0
The draws below stay inside these ranges and needn't reach their ends.
There are 2 independent parts, one for each index of `groups`. The reference program is written for one: setup_inputs(seed, part) draws one part's arguments, and reference() takes and returns one part's arrays. A program takes and returns all parts, laid end to end along the dimension named above; an argument that names none is the same for every part. Nothing has to cross between parts.
Inputs may be any that keep to these rules, and one draw needn't show every extreme that they name: `tile_list`: slot 0 of every list is the query tile itself; the 16 slots of a list name distinct tiles.
All inputs are finite; a program needn't handle non-finite values.
Results may differ from the reference program's by a relative error of at most 0.0047.
Values may be sent and summed in bfloat16 or wider, within the bound.
A program may use at most 192 MiB of HBM per device.

```python
import jax
import jax.numpy as jnp
from jax import lax

D = 3072
HEADS = 24
REQS = 4
WINDOW = 16
TILES = 16
SEQ_LEN = 4096


def draw_queries(key, part):
    key = jax.random.fold_in(key, 1)
    base = jnp.clip(jax.random.normal(key, (REQS, SEQ_LEN, D), jnp.float32), -6.0, 6.0)
    return base.astype(jnp.bfloat16)


def draw_keys(key, part):
    key = jax.random.fold_in(key, 2)
    base = jnp.clip(jax.random.normal(key, (REQS, SEQ_LEN, D), jnp.float32), -6.0, 6.0)
    return base.astype(jnp.bfloat16)


def draw_tile_list(key, part):
    key = jax.random.fold_in(key, 3)
    noise = jax.random.randint(key, (HEADS, TILES, TILES), 0, 4, jnp.int32)
    query_tile = jnp.arange(TILES, dtype=jnp.int32)[None, :, None]
    key_tile = jnp.arange(TILES, dtype=jnp.int32)[None, None, :]
    score = (noise + jnp.abs(key_tile - query_tile)) * TILES + key_tile
    score = jnp.where(key_tile == query_tile, -1, score)
    return jnp.argsort(score, axis=-1)[:, :, :WINDOW].astype(jnp.int32)


def draw_head_counts(key, part):
    key = jax.random.fold_in(key, 4)
    counts = jax.random.randint(key, (HEADS,), 4, WINDOW - 1, jnp.int32)
    chosen = jax.random.permutation(jax.random.fold_in(key, 5), HEADS)
    counts = counts.at[chosen[0]].set(WINDOW)
    counts = counts.at[chosen[1]].set(4)
    return counts.astype(jnp.int32)


def levels(stream_key, extent, split, least, high):
    loudness, own = 1.0, jax.random.fold_in(stream_key, 6)
    for dim, shards_of in split:
        heights = jnp.exp(jax.random.uniform(jax.random.fold_in(own, dim), (shards_of,), jnp.float32, least / len(split), high / len(split)))
        loudness = loudness * jnp.repeat(heights, extent[dim] // shards_of).reshape([-1 if axis == dim else 1 for axis in range(len(extent))])
    return loudness


def gaussian(rng, shape, scale, most, split=(), held_as=jnp.bfloat16):
    drawn = scale * jax.random.normal(rng, shape, jnp.float32)
    if split:
        drawn = drawn * levels(rng, shape, split, -0.22, 0.18)
    return jnp.clip(drawn, -most, most).astype(held_as)


def setup_inputs(seed: int = 0, part: int = 0) -> dict:
    seeds = jax.random.split(jax.random.key(seed), 6)
    part_splits = jax.random.split(jax.random.fold_in(seeds[5], part), 6)
    return {
        "queries": draw_queries(jax.random.fold_in(jax.random.fold_in(seeds[5], part), 71), part),
        "keys": draw_keys(jax.random.fold_in(jax.random.fold_in(seeds[5], part), 71), part),
        "values": gaussian(part_splits[2], (REQS, SEQ_LEN, D), 1.0, 6.0, ((1, 16),)),
        "tile_list": draw_tile_list(jax.random.fold_in(seeds[5], 71), part),
        "head_counts": draw_head_counts(jax.random.fold_in(seeds[5], 71), part),
    }


def to_tasks(array, heads):
    reqs, length, width = array.shape
    return array.reshape(reqs, length, heads, width // heads).transpose(0, 2, 1, 3).reshape(reqs * heads, length, width // heads)


def from_tasks(array, reqs):
    tasks, length, head_width = array.shape
    heads = tasks // reqs
    return array.reshape(reqs, heads, length, head_width).transpose(0, 2, 1, 3).reshape(reqs, length, heads * head_width)


def attend(query_task, key_task, value_task, lists, count):
    tiles = lists.shape[0]
    length, width = query_task.shape
    tile_rows = length // tiles
    query_blocks = query_task.astype(jnp.float32).reshape(tiles, tile_rows, width)
    key_blocks = key_task.astype(jnp.float32).reshape(tiles, tile_rows, width)
    value_blocks = value_task.astype(jnp.float32).reshape(tiles, tile_rows, width)
    factor = width ** -0.5

    def advance(slot, carry):
        running, total, accum = carry
        picked = lax.dynamic_index_in_dim(lists, slot, 1, keepdims=False).astype(jnp.int32)
        key_tiles = jnp.take(key_blocks, picked, axis=0)
        value_tiles = jnp.take(value_blocks, picked, axis=0)
        scores = jnp.einsum("tqd,tkd->tqk", query_blocks, key_tiles) * factor
        newmax = jnp.maximum(running, jnp.max(scores, axis=-1))
        carried = jnp.exp(running - newmax)
        weights = jnp.exp(scores - newmax[..., None])
        total = carried * total + jnp.sum(weights, axis=-1)
        rounded = lax.optimization_barrier(weights.astype(jnp.bfloat16)).astype(jnp.float32)
        accum = carried[..., None] * accum + jnp.einsum("tqk,tkd->tqd", rounded, value_tiles)
        return newmax, total, accum

    start = (jnp.full((tiles, tile_rows), -1e30, jnp.float32),
             jnp.zeros((tiles, tile_rows), jnp.float32),
             jnp.zeros((tiles, tile_rows, width), jnp.float32))
    running, total, accum = lax.fori_loop(0, count, advance, start)
    return (accum / total[..., None]).astype(jnp.bfloat16).reshape(length, width)


def reference(queries, keys, values, tile_list, head_counts):
    query_tasks = to_tasks(queries, HEADS)
    key_tasks = to_tasks(keys, HEADS)
    value_tasks = to_tasks(values, HEADS)
    lists_rep = jnp.tile(tile_list, (REQS, 1, 1))
    counts_rep = jnp.tile(head_counts, REQS)
    outputs = lax.map(lambda items: attend(*items), (query_tasks, key_tasks, value_tasks, lists_rep, counts_rep))
    return from_tasks(outputs, REQS)
```

```python
import functools

import jax
import jax.numpy as jnp
from jax import lax
from jax.experimental import pallas as pl
from jax.experimental.pallas import tpu as pltpu
from jax.sharding import PartitionSpec as P

GROUP = 4
CHUNKS = 3
LOG2E = 1.4426950408889634


def place(p, j, devices):
    return j * devices + (p if j % 2 == 0 else devices - 1 - p)


def pack_kernel(slots, reqs, order, queries, keys, values, out, sem):
    devices = out.shape[0]
    length, width = out.shape[3:]
    copies = []
    for here, j in enumerate(slots):
        for p in range(devices):
            rank = place(p, j, devices)
            head = order[rank // reqs]
            columns = pl.ds(pl.multiple_of(head * width, width), width)
            for which, array in enumerate((queries, keys, values)):
                copies.append(
                    pltpu.make_async_copy(
                        array.at[rank % reqs, :, columns],
                        out.at[p, here, which],
                        sem.at[len(copies)],
                    )
                )
    for copy in copies:
        copy.start()
    for copy in copies:
        copy.wait()


def unpack_kernel(chunks, reqs, order, *refs):
    arrays, out, sem = refs[: len(chunks)], refs[-2], refs[-1]
    devices, _, length, width = arrays[0].shape
    copies = []
    for slots, array in zip(chunks, arrays):
        for here, j in enumerate(slots):
            for p in range(devices):
                rank = place(p, j, devices)
                head = order[rank // reqs]
                columns = pl.ds(pl.multiple_of(head * width, width), width)
                copies.append(
                    pltpu.make_async_copy(
                        array.at[p, here],
                        out.at[rank % reqs, :, columns],
                        sem.at[len(copies)],
                    )
                )
    for copy in copies:
        copy.start()
    for copy in copies:
        copy.wait()


def attend_kernel(window, owned, counts, lists, data, out, turned):
    tiles = data.shape[0]
    rows, width = data.shape[3:]
    head = owned[pl.program_id(0)]
    count = counts[head]
    group = GROUP if tiles % GROUP == 0 else 1
    factor = width ** (-0.5) * LOG2E

    @pl.loop(0, tiles)
    def turn(tile):
        turned[tile, :width, :] = data[tile, 0, 2].T
        turned[tile, width:, :] = jnp.ones((16, rows), jnp.bfloat16)

    @pl.loop(0, tiles // group)
    def some_tiles(block):
        first = block * group
        bases = [(head * tiles + first + g) * window for g in range(group)]

        def advance(slot, carry):
            result = []
            for g in range(group):
                running, accum = carry[g]
                picked = lists[bases[g] + slot]
                scores = lax.dot_general(
                    data[picked, 0, 1],
                    data[first + g, 0, 0],
                    (((1,), (1,)), ((), ())),
                    preferred_element_type=jnp.float32,
                )
                newmax = jnp.maximum(running, jnp.max(scores, axis=0, keepdims=True) * factor)
                carried = jnp.exp2(running - newmax)
                weights = jnp.exp2(scores * factor - newmax).astype(jnp.bfloat16)
                accum = carried * accum + jnp.dot(
                    turned[picked], weights, preferred_element_type=jnp.float32
                )
                result.append((newmax, accum))
            return tuple(result)

        start = tuple(
            (
                jnp.full((1, rows), -1e30, jnp.float32),
                jnp.zeros((width + 16, rows), jnp.float32),
            )
            for _ in range(group)
        )
        done = lax.fori_loop(0, count, advance, start)
        for g in range(group):
            accum = done[g][1]
            ratio = accum[:width] / accum[width : width + 1]
            out[first + g, 0] = ratio.T.astype(jnp.bfloat16)


def on_device(queries, keys, values, tile_list, head_counts):
    reqs, rows, model_width = queries.shape
    heads = head_counts.shape[0]
    window = tile_list.shape[2]
    width = model_width // heads
    devices = lax.axis_size("seq")
    tasks = reqs * heads
    per_device = tasks // devices
    me = lax.axis_index("seq")
    each = -(-per_device // CHUNKS)
    chunks = [
        tuple(range(begin, min(begin + each, per_device)))
        for begin in range(0, per_device, each)
    ]

    ids = jnp.arange(heads, dtype=jnp.int32)
    mine, other = head_counts[:, None], head_counts[None, :]
    ahead = (other > mine) | ((other == mine) & (ids[None, :] < ids[:, None]))
    ranks = jnp.sum(ahead.astype(jnp.int32), axis=1)
    order = jnp.sum(jnp.where(ranks[None, :] == ids[:, None], ids[None, :], 0), axis=1)

    lists = lax.all_gather(tile_list, "seq", axis=1, tiled=True).reshape(-1)

    smem = pl.BlockSpec(memory_space=pltpu.SMEM)
    hbm = pl.BlockSpec(memory_space=pl.ANY)
    arrived = []
    for slots in chunks:
        packed = pl.pallas_call(
            functools.partial(pack_kernel, slots, reqs),
            out_shape=jax.ShapeDtypeStruct((devices, len(slots), 3, rows, width), jnp.bfloat16),
            in_specs=[smem, hbm, hbm, hbm],
            out_specs=hbm,
            scratch_shapes=[pltpu.SemaphoreType.DMA((3 * devices * len(slots),))],
        )(order, queries, keys, values)
        arrived.append(lax.all_to_all(packed, "seq", split_axis=0, concat_axis=0, tiled=True))

    returned = []
    for slots, data in zip(chunks, arrived):
        spots = jnp.stack(
            [place(me, j, devices) // reqs for j in slots]
        )
        owned = jnp.sum(jnp.where(spots[:, None] == ids[None, :], order[None, :], 0), axis=1)
        count = len(slots)
        done = pl.pallas_call(
            functools.partial(attend_kernel, window),
            out_shape=jax.ShapeDtypeStruct((devices, count, rows, width), jnp.bfloat16),
            grid_spec=pltpu.PrefetchScalarGridSpec(
                num_scalar_prefetch=3,
                grid=(count,),
                in_specs=[
                    pl.BlockSpec((devices, 1, 3, rows, width), lambda i, *_: (0, i, 0, 0, 0))
                ],
                out_specs=pl.BlockSpec((devices, 1, rows, width), lambda i, *_: (0, i, 0, 0)),
                scratch_shapes=[pltpu.VMEM((devices, width + 16, rows), jnp.bfloat16)],
            ),
            compiler_params=pltpu.CompilerParams(vmem_limit_bytes=40 * 1024 * 1024),
            cost_estimate=pl.CostEstimate(
                flops=count * devices * 10 * 4 * rows * rows * width,
                bytes_accessed=count * devices * 4 * rows * width * 2,
                transcendentals=count * devices * 10 * rows * rows,
            ),
        )(owned, head_counts, lists, data)
        returned.append(lax.all_to_all(done, "seq", split_axis=0, concat_axis=0, tiled=True))

    return pl.pallas_call(
        functools.partial(unpack_kernel, chunks, reqs),
        out_shape=jax.ShapeDtypeStruct(queries.shape, jnp.bfloat16),
        in_specs=[smem] + [hbm] * len(chunks),
        out_specs=hbm,
        scratch_shapes=[pltpu.SemaphoreType.DMA((tasks,))],
    )(order, *returned)


def solution(mesh):
    in_specs = (
        P("groups", "seq", None),
        P("groups", "seq", None),
        P("groups", "seq", None),
        P(None, "seq", None),
        P(),
    )
    out_specs = P("groups", "seq", None)
    return jax.shard_map(
        on_device, mesh=mesh, in_specs=in_specs, out_specs=out_specs, check_vma=False
    )
```

```python
import functools

import jax
import jax.numpy as jnp
from jax import lax
from jax.experimental import pallas as pl
from jax.experimental.pallas import tpu as pltpu
from jax.sharding import PartitionSpec as P

GROUP = 4
LOG2E = 1.4426950408889634


def pick(group, j, groups):
    return j * groups + (group if j % 2 == 0 else groups - 1 - group)


def pick_traced(group, j, groups):
    return j * groups + jnp.where(j % 2 == 0, group, groups - 1 - group)


def pack_kernel(order, queries, keys, values, before, out):
    out[:, 0, 0] = queries[...]
    out[:, 0, 1] = keys[...]
    out[:, 0, 2] = values[...]


def unpack_kernel(order, *refs):
    out = refs[-1]
    for chunk, array in enumerate(refs[:-1]):

        @pl.when(pl.program_id(0) == chunk)
        def store():
            out[...] = array[:, 0]


def attend_kernel(window, owned, counts, lists, data, before, out, turned, columns):
    tiles = data.shape[0]
    rows, width = data.shape[3:]
    head = owned[pl.program_id(0)]
    count = counts[head]
    group = GROUP if tiles % GROUP == 0 else 1
    factor = width ** (-0.5) * LOG2E

    @pl.loop(0, tiles)
    def turn(tile):
        turned[tile, :width, :] = data[tile, 0, 2].T
        turned[tile, width:, :] = jnp.ones((16, rows), jnp.bfloat16)
        columns[tile] = data[tile, 0, 0].T

    @pl.loop(0, tiles // group)
    def some_tiles(block):
        first = block * group
        bases = [(head * tiles + first + g) * window for g in range(group)]

        def advance(slot, carry):
            result = []
            for g in range(group):
                running, accum = carry[g]
                picked = lists[bases[g] + slot]
                scores = jnp.dot(
                    data[picked, 0, 1], columns[first + g], preferred_element_type=jnp.float32
                )
                newmax = jnp.maximum(running, jnp.max(scores, axis=0, keepdims=True) * factor)
                carried = jnp.exp2(running - newmax)
                weights = jnp.exp2(scores * factor - newmax).astype(jnp.bfloat16)
                accum = carried * accum + jnp.dot(
                    turned[picked], weights, preferred_element_type=jnp.float32
                )
                result.append((newmax, accum))
            return tuple(result)

        start = tuple(
            (
                jnp.full((1, rows), -1e30, jnp.float32),
                jnp.zeros((width + 16, rows), jnp.float32),
            )
            for _ in range(group)
        )
        done = lax.fori_loop(0, count, advance, start)
        for g in range(group):
            accum = done[g][1]
            ratio = accum[:width] / accum[width : width + 1]
            out[first + g, 0] = ratio.T.astype(jnp.bfloat16)


def on_device(queries, keys, values, tile_list, head_counts):
    reqs, rows, model_width = queries.shape
    heads = head_counts.shape[0]
    window = tile_list.shape[2]
    width = model_width // heads
    devices = lax.axis_size("seq")
    tasks = reqs * heads
    per_device = tasks // devices
    groups = devices // reqs
    me = lax.axis_index("seq")
    each = 1
    starts = range(0, per_device, each)

    ids = jnp.arange(heads, dtype=jnp.int32)
    mine, other = head_counts[:, None], head_counts[None, :]
    ahead = (other > mine) | ((other == mine) & (ids[None, :] < ids[:, None]))
    ranks = jnp.sum(ahead.astype(jnp.int32), axis=1)
    order = jnp.sum(jnp.where(ranks[None, :] == ids[:, None], ids[None, :], 0), axis=1)

    lists = lax.all_gather(tile_list, "seq", axis=1, tiled=True).reshape(-1)
    order, lists = lax.optimization_barrier((order, lists))

    hbm = pl.BlockSpec(memory_space=pl.ANY)

    def from_head(begin):
        def index(g, i, order):
            return (0, 0, order[pick_traced(g, begin + i, groups)])

        return pl.BlockSpec((reqs, rows, width), index)

    def send(begin, before):
        packed = pl.pallas_call(
            pack_kernel,
            out_shape=jax.ShapeDtypeStruct((devices, each, 3, rows, width), jnp.bfloat16),
            grid_spec=pltpu.PrefetchScalarGridSpec(
                num_scalar_prefetch=1,
                grid=(groups, each),
                in_specs=[from_head(begin)] * 3 + [hbm],
                out_specs=pl.BlockSpec(
                    (reqs, 1, 3, rows, width), lambda g, i, *_: (g, i, 0, 0, 0)
                ),
            ),
        )(order, queries, keys, values, before)
        return packed, lax.all_to_all(packed, "seq", split_axis=0, concat_axis=0, tiled=True)

    returned = []
    done = order
    packed, following = send(0, order)
    for begin in starts:
        data = following
        if begin + 1 < per_device:
            packed, following = send(begin + 1, done if begin else packed)
        spots = jnp.stack([pick(me // reqs, begin + i, groups) for i in range(each)])
        owned = jnp.sum(jnp.where(spots[:, None] == ids[None, :], order[None, :], 0), axis=1)
        done = pl.pallas_call(
            functools.partial(attend_kernel, window),
            out_shape=jax.ShapeDtypeStruct((devices, each, rows, width), jnp.bfloat16),
            grid_spec=pltpu.PrefetchScalarGridSpec(
                num_scalar_prefetch=3,
                grid=(each,),
                in_specs=[
                    pl.BlockSpec((devices, 1, 3, rows, width), lambda i, *_: (0, i, 0, 0, 0)),
                    hbm,
                ],
                out_specs=pl.BlockSpec((devices, 1, rows, width), lambda i, *_: (0, i, 0, 0)),
                scratch_shapes=[
                    pltpu.VMEM((devices, width + 16, rows), jnp.bfloat16),
                    pltpu.VMEM((devices, width, rows), jnp.bfloat16),
                ],
            ),
            compiler_params=pltpu.CompilerParams(vmem_limit_bytes=40 * 1024 * 1024),
            cost_estimate=pl.CostEstimate(
                flops=each * devices * 20 * 4 * rows * rows * width,
                bytes_accessed=each * devices * 4 * rows * width * 2,
                transcendentals=each * devices * 10 * rows * rows,
            ),
        )(owned, head_counts, lists, data, done)
        returned.append(lax.all_to_all(done, "seq", split_axis=0, concat_axis=0, tiled=True))

    def from_chunk(chunk):
        def index(c, i, g, order):
            now = c == chunk
            last = c > chunk
            hold = jnp.where(last, groups - 1, 0)
            return (jnp.where(now, g, hold), jnp.where(now, i, jnp.where(last, each - 1, 0)), 0, 0)

        return pl.BlockSpec((reqs, 1, rows, width), index)

    return pl.pallas_call(
        unpack_kernel,
        out_shape=jax.ShapeDtypeStruct(queries.shape, jnp.bfloat16),
        grid_spec=pltpu.PrefetchScalarGridSpec(
            num_scalar_prefetch=1,
            grid=(len(starts), each, groups),
            in_specs=[from_chunk(chunk) for chunk in range(len(starts))],
            out_specs=pl.BlockSpec(
                (reqs, rows, width),
                lambda c, i, g, order: (0, 0, order[pick_traced(g, c * each + i, groups)]),
            ),
        ),
    )(order, *returned)


def solution(mesh):
    in_specs = (
        P("groups", "seq", None),
        P("groups", "seq", None),
        P("groups", "seq", None),
        P(None, "seq", None),
        P(),
    )
    out_specs = P("groups", "seq", None)
    return jax.shard_map(
        on_device, mesh=mesh, in_specs=in_specs, out_specs=out_specs, check_vma=False
    )
```

```python
import functools

import jax
import jax.numpy as jnp
from jax import lax
from jax.experimental import pallas as pl
from jax.experimental.pallas import tpu as pltpu
from jax.sharding import PartitionSpec as P

GROUP = 4
LOG2E = 1.4426950408889634


def pick(group, j, groups):
    return j * groups + (group if j % 2 == 0 else groups - 1 - group)


def pick_traced(group, j, groups):
    return j * groups + jnp.where(j % 2 == 0, group, groups - 1 - group)


def pack_kernel(order, queries, keys, values, before, out):
    out[:, 0, 0] = queries[...]
    out[:, 0, 1] = keys[...]
    out[:, 0, 2] = values[...]


def unpack_kernel(spans, order, *refs):
    out = refs[-1]
    now = pl.program_id(0)
    for (begin, end), array in zip(spans, refs[:-1]):

        @pl.when((now >= begin) & (now < end))
        def store():
            out[...] = array[:, 0]


def at_task(task, i, *_):
    return (0, task + i, 0, 0)


def attend_kernel(window, owned, counts, lists, data, before, ahead, out, turned, columns):
    tiles = data.shape[0]
    rows, width = data.shape[3:]
    head = owned[pl.program_id(0)]
    count = counts[head]
    group = GROUP if tiles % GROUP == 0 else 1
    factor = width ** (-0.5) * LOG2E

    @pl.loop(0, tiles)
    def turn(tile):
        turned[tile, :width, :] = data[tile, 0, 2].T
        turned[tile, width:, :] = jnp.ones((16, rows), jnp.bfloat16)
        columns[tile] = data[tile, 0, 0].T

    @pl.loop(0, tiles // group)
    def some_tiles(block):
        first = block * group
        bases = [(head * tiles + first + g) * window for g in range(group)]

        def advance(slot, carry):
            result = []
            for g in range(group):
                running, accum = carry[g]
                picked = lists[bases[g] + slot]
                scores = jnp.dot(
                    data[picked, 0, 1], columns[first + g], preferred_element_type=jnp.float32
                )
                newmax = jnp.maximum(running, jnp.max(scores, axis=0, keepdims=True) * factor)
                carried = jnp.exp2(running - newmax)
                weights = jnp.exp2(scores * factor - newmax).astype(jnp.bfloat16)
                accum = carried * accum + jnp.dot(
                    turned[picked], weights, preferred_element_type=jnp.float32
                )
                result.append((newmax, accum))
            return tuple(result)

        start = tuple(
            (
                jnp.full((1, rows), -1e30, jnp.float32),
                jnp.zeros((width + 16, rows), jnp.float32),
            )
            for _ in range(group)
        )
        done = lax.fori_loop(0, count, advance, start)
        for g in range(group):
            accum = done[g][1]
            ratio = accum[:width] / accum[width : width + 1]
            out[first + g, 0] = ratio.T.astype(jnp.bfloat16)


def on_device(queries, keys, values, tile_list, head_counts):
    reqs, rows, model_width = queries.shape
    heads = head_counts.shape[0]
    window = tile_list.shape[2]
    width = model_width // heads
    devices = lax.axis_size("seq")
    tasks = reqs * heads
    per_device = tasks // devices
    groups = devices // reqs
    me = lax.axis_index("seq")
    each = 1
    split = max(per_device - 1, 1)
    spans = [(0, split), (split, per_device)] if split < per_device else [(0, split)]

    ids = jnp.arange(heads, dtype=jnp.int32)
    mine, other = head_counts[:, None], head_counts[None, :]
    ahead = (other > mine) | ((other == mine) & (ids[None, :] < ids[:, None]))
    ranks = jnp.sum(ahead.astype(jnp.int32), axis=1)
    order = jnp.sum(jnp.where(ranks[None, :] == ids[:, None], ids[None, :], 0), axis=1)

    lists = lax.all_gather(tile_list, "seq", axis=1, tiled=True).reshape(-1)
    order, lists = lax.optimization_barrier((order, lists))

    hbm = pl.BlockSpec(memory_space=pl.ANY)

    def from_head(begin):
        def index(g, i, order):
            return (0, 0, order[pick_traced(g, begin + i, groups)])

        return pl.BlockSpec((reqs, rows, width), index)

    def send(begin, before):
        packed = pl.pallas_call(
            pack_kernel,
            out_shape=jax.ShapeDtypeStruct((devices, each, 3, rows, width), jnp.bfloat16),
            grid_spec=pltpu.PrefetchScalarGridSpec(
                num_scalar_prefetch=1,
                grid=(groups, each),
                in_specs=[from_head(begin)] * 3 + [hbm],
                out_specs=pl.BlockSpec(
                    (reqs, 1, 3, rows, width), lambda g, i, *_: (g, i, 0, 0, 0)
                ),
            ),
        )(order, queries, keys, values, before)
        return packed, lax.all_to_all(packed, "seq", split_axis=0, concat_axis=0, tiled=True)

    returned = []
    done = order
    packed, following = send(0, order)
    for step in range(per_device):
        data = following
        if step + 1 < per_device:
            packed, following = send(step + 1, done if step else packed)
        begin, end = spans[0] if step < split else spans[1]
        spots = jnp.stack([pick(me // reqs, step + i, groups) for i in range(each)])
        owned = jnp.sum(jnp.where(spots[:, None] == ids[None, :], order[None, :], 0), axis=1)
        done = pl.pallas_call(
            functools.partial(attend_kernel, window),
            out_shape=jax.ShapeDtypeStruct((devices, end - begin, rows, width), jnp.bfloat16),
            input_output_aliases={} if step == begin else {4: 0},
            grid_spec=pltpu.PrefetchScalarGridSpec(
                num_scalar_prefetch=3,
                grid=(each,),
                in_specs=[
                    pl.BlockSpec((devices, 1, 3, rows, width), lambda i, *_: (0, i, 0, 0, 0)),
                    hbm,
                    hbm,
                ],
                out_specs=pl.BlockSpec(
                    (devices, 1, rows, width), functools.partial(at_task, step - begin)
                ),
                scratch_shapes=[
                    pltpu.VMEM((devices, width + 16, rows), jnp.bfloat16),
                    pltpu.VMEM((devices, width, rows), jnp.bfloat16),
                ],
            ),
            compiler_params=pltpu.CompilerParams(vmem_limit_bytes=40 * 1024 * 1024),
            cost_estimate=pl.CostEstimate(
                flops=each * devices * 20 * 4 * rows * rows * width,
                bytes_accessed=each * devices * 4 * rows * width * 2,
                transcendentals=each * devices * 10 * rows * rows,
            ),
        )(owned, head_counts, lists, data, done, packed)
        if step + 1 == end:
            returned.append(
                lax.all_to_all(done, "seq", split_axis=0, concat_axis=0, tiled=True)
            )

    def from_span(begin, end):
        def index(j, g, order):
            before, after = j < begin, j >= end
            row = jnp.where(before, 0, jnp.where(after, groups - 1, g))
            return (row, jnp.clip(j - begin, 0, end - begin - 1), 0, 0)

        return pl.BlockSpec((reqs, 1, rows, width), index)

    return pl.pallas_call(
        functools.partial(unpack_kernel, spans),
        out_shape=jax.ShapeDtypeStruct(queries.shape, jnp.bfloat16),
        grid_spec=pltpu.PrefetchScalarGridSpec(
            num_scalar_prefetch=1,
            grid=(per_device, groups),
            in_specs=[from_span(begin, end) for begin, end in spans],
            out_specs=pl.BlockSpec(
                (reqs, rows, width),
                lambda j, g, order: (0, 0, order[pick_traced(g, j, groups)]),
            ),
        ),
    )(order, *returned)


def solution(mesh):
    in_specs = (
        P("groups", "seq", None),
        P("groups", "seq", None),
        P("groups", "seq", None),
        P(None, "seq", None),
        P(),
    )
    out_specs = P("groups", "seq", None)
    return jax.shard_map(
        on_device, mesh=mesh, in_specs=in_specs, out_specs=out_specs, check_vma=False
    )
```
